256 devices in a mesh: gossip: 32 (over z_lo, x, core), tensor: 8 (over z_hi, y).
Axes of the slice: x: 4, y: 4, z: 8 (z_hi: 2, z_lo: 4; z = z_hi * 4 + z_lo), core: 2. Of those that a mesh axis runs over, the one named last changes fastest.
Arguments:
- weights: float32 [32, 8192, 1024], P('gossip', 'tensor'), may hold values from -6 to 6
- updates: bfloat16 [32, 2, 8192, 1024], P('gossip', None, 'tensor'), may hold values from -4 to 4
- factors: bfloat16 [3, 1024, 128], replicated, may hold values from -6 to 6
- partners: int32 [3, 32], replicated, may hold values from 0 to 31, as said below
Outputs:
- averaged: float32 [32, 8192, 1024], P('gossip', 'tensor')
The draws below stay inside these ranges and needn't reach their ends.
Inputs may be any that keep to these rules, and one draw needn't show every extreme that they name: Row k pairs replica i with replica i XOR c_k, for one offset c_k of 1 to 31 a row; so each row is a perfect matching and partners[k, partners[k, i]] = i.
All inputs are finite; a program needn't handle non-finite values.
Results may differ from the reference program's by a relative error of at most 0.0003.
Values sent between devices are 32-bit elements; how exact they have to be, the bound alone decides.
A program may use at most 64 MiB of HBM per device.

```python
import jax
import jax.numpy as jnp
from jax import lax

D = 8192
KV = 1024
RANK = 128
MATCHINGS = 3
REPLICAS = 32
N_GOSSIP = 32


def draw_partners(key, part):
    offsets = jax.random.randint(jax.random.fold_in(key, 17), (MATCHINGS, 1), 1, N_GOSSIP)
    indices = jnp.arange(N_GOSSIP, dtype=jnp.int32)[None, :]
    return jnp.bitwise_xor(indices, offsets.astype(jnp.int32)).astype(jnp.int32)


def block_levels(rng, dims, shards, smallest, largest):
    level, own = 1.0, jax.random.fold_in(rng, 6)
    for position, parts in shards:
        steps = jnp.exp(jax.random.uniform(jax.random.fold_in(own, position), (parts,), jnp.float32, smallest / len(shards), largest / len(shards)))
        level = level * jnp.repeat(steps, dims[position] // parts).reshape([-1 if axis == position else 1 for axis in range(len(dims))])
    return level


def normal_values(rng, extent, scale, reach, cuts=(), kind=jnp.bfloat16):
    entries = jax.random.normal(rng, extent, jnp.float32) * scale
    if len(cuts) > 0:
        entries = block_levels(rng, extent, cuts, -0.22, 0.18) * entries
    return jnp.clip(entries, min=-reach, max=reach).astype(kind)


def setup_inputs(seed: int = 0) -> dict:
    streams_of = jax.random.split(jax.random.key(seed), 5)
    return {
        "weights": normal_values(streams_of[0], (REPLICAS, D, KV), 1.0, 6.0, ((0, 32), (1, 8)), jnp.float32),
        "updates": normal_values(streams_of[1], (REPLICAS, MATCHINGS - 1, D, KV), 0.5, 4.0, ((0, 32), (2, 8))),
        "factors": normal_values(streams_of[2], (MATCHINGS, KV, RANK), 1.0, 6.0),
        "partners": draw_partners(jax.random.fold_in(streams_of[4], 71), 0),
    }


def orthonormal(factor_low, left_block):
    return jax.scipy.linalg.solve_triangular(factor_low, left_block.T, lower=True).T

def reference(weights, updates, factors, partners):
    highest = lax.Precision.HIGHEST
    replicas = weights
    for matching in range(MATCHINGS):
        if matching > 0:
            replicas = replicas - updates[:, matching - 1].astype(jnp.float32)
        right_start = factors[matching].astype(jnp.float32)
        partner_ids = partners[matching].astype(jnp.int32)
        own_left = jnp.einsum('rdk,kq->rdq', replicas, right_start, precision=highest)
        left_block = own_left - own_left[partner_ids]
        gram_total = jnp.einsum('rdq,rdp->rqp', left_block, left_block, precision=highest)
        factor_low = jax.vmap(jnp.linalg.cholesky)(gram_total)
        ortho = jax.vmap(orthonormal)(factor_low, left_block)
        partial_value = jnp.einsum('rdk,rdq->rkq', replicas, ortho, precision=highest)
        right_total = partial_value + partial_value[partner_ids]
        replicas = replicas - 0.5 * jnp.einsum('rdq,rkq->rdk', ortho, right_total, precision=highest)
    return replicas
```

```python
import functools

import jax
import jax.numpy as jnp
from jax import lax
from jax.experimental import pallas as pl
from jax.experimental.pallas import tpu as pltpu
from jax.sharding import PartitionSpec as P

MATCHINGS = 3
CHUNKS = 4
RING = 4
HIGHEST = lax.Precision.HIGHEST
F32 = jnp.float32
BF16 = jnp.bfloat16


def halves(value):
    high = value.astype(BF16)
    return high, (value - high.astype(F32)).astype(BF16)


def dot(first, second, first_dim, second_dim, precision=None):
    return lax.dot_general(
        first,
        second,
        (((first_dim,), (second_dim,)), ((), ())),
        precision=precision,
        preferred_element_type=F32,
    )


def flipped(index, offset):
    bit = 1
    result = index
    while bit <= offset:
        if offset & bit:
            result = result + bit * (1 - 2 * ((index // bit) % 2))
        bit *= 2
    return result


def eliminated(matrix, pivots):
    size = matrix.shape[0]
    lane = lax.broadcasted_iota(jnp.int32, (1, size), 1)
    row_id = lax.broadcasted_iota(jnp.int32, (size, 1), 0)
    for k in range(pivots):
        pivot = 1.0 / matrix[k : k + 1, k : k + 1]
        row = jnp.where(lane == k, pivot, matrix[k : k + 1, :] * pivot)
        column = jnp.where(row_id == k, -1.0, matrix[:, k : k + 1])
        kept = jnp.where((lane == k) | (row_id == k), 0.0, matrix)
        matrix = kept - column * row
    return pltpu.roll(pltpu.roll(matrix, size - pivots, 0), size - pivots, 1)


def phase_kernel(
    offset,
    own,
    w_hbm,
    xt,
    st,
    wf,
    whi,
    wlo,
    theirs,
    rp,
    yr,
    zs,
    zr,
    ps,
    pr,
    rf,
    gp,
    gy,
    gzs,
    gz,
    gf,
    inv,
    w_sem,
    e_send,
    e_recv,
    y_send,
    y_recv,
    z_send,
    z_recv,
    p_send,
    p_recv,
    a_send,
    a_recv,
    gy_send,
    gy_recv,
    gz_send,
    gz_recv,
    ga_send,
    ga_recv,
):
    rank, depth = own.shape
    quarter = rp.shape[2]
    part = rank // CHUNKS
    gpart = rank // RING
    g, t = lax.axis_index("gossip"), lax.axis_index("tensor")
    y, zh = t % RING, t // RING
    around = [zh * RING + (y + i) % RING for i in range(RING)]
    across = (1 - zh) * RING + y
    mate = flipped(g, offset)

    load_w = pltpu.make_async_copy(w_hbm, wf, w_sem)
    load_w.start()

    barrier = pltpu.get_barrier_semaphore()
    for device in [(g, around[1]), (g, around[2]), (g, around[3]), (g, across), (mate, t)]:
        pl.semaphore_signal(barrier, inc=1, device_id=device, device_id_type=pl.DeviceIdType.MESH)
    pl.semaphore_wait(barrier, 5)

    def rows(j):
        return pl.ds(j * part, part)

    def remote(src, dst, send, recv, device):
        return pltpu.make_async_remote_copy(
            src_ref=src,
            dst_ref=dst,
            send_sem=send,
            recv_sem=recv,
            device_id=device,
            device_id_type=pl.DeviceIdType.MESH,
        )

    e_copy = [
        remote(own.at[rows(j)], theirs.at[rows(j)], e_send.at[j], e_recv.at[j], (mate, t))
        for j in range(CHUNKS)
    ]
    y_copy = [
        [
            remote(
                rp.at[(y + i) % RING, rows(j)],
                yr.at[i - 1, rows(j)],
                y_send.at[j, i - 1],
                y_recv.at[j, i - 1],
                (g, around[i]),
            )
            for i in range(1, RING)
        ]
        for j in range(CHUNKS)
    ]
    z_copy = [
        remote(zs.at[rows(j)], zr.at[rows(j)], z_send.at[j], z_recv.at[j], (g, across))
        for j in range(CHUNKS)
    ]
    p_copy = [
        remote(ps.at[rows(j)], pr.at[rows(j)], p_send.at[j], p_recv.at[j], (mate, t))
        for j in range(CHUNKS)
    ]
    a_copy = [
        [
            remote(
                rf.at[y, rows(j)],
                rf.at[y, rows(j)],
                a_send.at[j, i - 1],
                a_recv.at[j, i - 1],
                (g, around[i]),
            )
            for i in range(1, RING)
        ]
        for j in range(CHUNKS)
    ]
    gy_copy = [
        remote(
            gp.at[(y + i) % RING], gy.at[i - 1], gy_send.at[i - 1], gy_recv.at[i - 1], (g, around[i])
        )
        for i in range(1, RING)
    ]
    gz_copy = remote(gzs, gz, gz_send, gz_recv, (g, across))
    ga_copy = [
        remote(gf.at[y], gf.at[y], ga_send.at[i - 1], ga_recv.at[i - 1], (g, around[i]))
        for i in range(1, RING)
    ]

    for copy in e_copy:
        copy.start()

    load_w.wait()
    strip = 128

    @pl.loop(0, depth // strip)
    def _(s):
        at = pl.ds(pl.multiple_of(s * strip, strip), strip)
        for n in range(RING):
            high, low = halves(wf[at, n * quarter : (n + 1) * quarter])
            whi[n, at, :] = high
            wlo[n, at, :] = low

    def gram():
        total = dot(xt[...], xt[...], 1, 1, HIGHEST)
        for n in range(RING):
            gp[n] = total[n * gpart : (n + 1) * gpart]
        for copy in gy_copy:
            copy.start()

    def right(j):
        high, low = halves(xt[rows(j)])
        both = jnp.concatenate([high, low], axis=0)
        for i in (2, 1, 3, 0):
            n = (y + i) % RING
            wide = dot(both, whi[n], 1, 0)
            rp[n, rows(j)] = wide[:part] + wide[part:] + dot(high, wlo[n], 1, 0)
            if i:
                y_copy[j][i - 1].start()

    def over_z(j):
        for copy in y_copy[j]:
            copy.wait_recv()
        zs[rows(j)] = (rp[y, rows(j)] + yr[0, rows(j)]) + (yr[1, rows(j)] + yr[2, rows(j)])
        z_copy[j].start()

    def with_mate(j):
        z_copy[j].wait_recv()
        ps[rows(j)] = zs[rows(j)] + zr[rows(j)]
        p_copy[j].start()

    def gather(j):
        p_copy[j].wait_recv()
        rf[y, rows(j)] = ps[rows(j)] + pr[rows(j)]
        for copy in a_copy[j]:
            copy.start()

    def gram_z():
        for copy in gy_copy:
            copy.wait_recv()
        gzs[...] = (gp[y] + gy[0]) + (gy[1] + gy[2])
        gz_copy.start()

    def gram_gather():
        gz_copy.wait_recv()
        gf[y] = gzs[...] + gz[...]
        for copy in ga_copy:
            copy.start()

    def invert(steps):
        inv[...] = lax.fori_loop(0, steps, lambda _, m: eliminated(m, rank // 8), inv[...])

    for j in range(CHUNKS):
        e_copy[j].wait_recv()
        xt[rows(j)] = own[rows(j)] - theirs[rows(j)]
        if j == CHUNKS - 1:
            gram()
        right(j)
        if j >= 1 and j < CHUNKS - 1:
            over_z(j - 1)
        if j >= 2 and j < CHUNKS - 1:
            with_mate(j - 2)
        if j >= 3 and j < CHUNKS - 1:
            gather(j - 3)
    last = CHUNKS - 1
    gram_z()
    if last >= 1:
        over_z(last - 1)
    if last >= 2:
        with_mate(last - 2)
    if last >= 3:
        gather(last - 3)
    gram_gather()
    over_z(last)
    if last >= 1:
        with_mate(last - 1)
    if last >= 2:
        gather(last - 2)
    for copy in ga_copy:
        copy.wait_recv()
    for n in range(RING):
        inv[n * gpart : (n + 1) * gpart] = gf[n]
    invert(3)
    with_mate(last)
    if last >= 1:
        gather(last - 1)
    invert(3)
    gather(last)
    invert(2)
    for j in range(CHUNKS):
        for copy in a_copy[j]:
            copy.wait_recv()
    for n in range(RING):
        st[:, n * quarter : (n + 1) * quarter] = dot(inv[...], rf[n], 1, 0, HIGHEST)

    for j in range(CHUNKS):
        e_copy[j].wait_send()
        z_copy[j].wait_send()
        p_copy[j].wait_send()
        for copy in y_copy[j] + a_copy[j]:
            copy.wait_send()
    gz_copy.wait_send()
    for copy in gy_copy + ga_copy:
        copy.wait_send()


def phase(offset, own, replica):
    rank, depth = own.shape
    width = replica.shape[1]
    quarter = width // RING
    gpart = rank // RING
    dma = pltpu.SemaphoreType.DMA
    vmem = pltpu.VMEM
    copies = [(CHUNKS,), (CHUNKS, 3), (CHUNKS,), (CHUNKS,), (CHUNKS, 3), (3,), (), (3,)]
    return pl.pallas_call(
        functools.partial(phase_kernel, offset),
        out_shape=(
            jax.ShapeDtypeStruct((rank, depth), F32),
            jax.ShapeDtypeStruct((rank, width), F32),
        ),
        in_specs=[pl.BlockSpec(memory_space=vmem), pl.BlockSpec(memory_space=pl.ANY)],
        out_specs=[pl.BlockSpec(memory_space=vmem), pl.BlockSpec(memory_space=vmem)],
        scratch_shapes=[
            vmem((depth, width), F32),
            vmem((RING, depth, quarter), BF16),
            vmem((RING, depth, quarter), BF16),
            vmem((rank, depth), F32),
            vmem((RING, rank, quarter), F32),
            vmem((RING - 1, rank, quarter), F32),
            vmem((rank, quarter), F32),
            vmem((rank, quarter), F32),
            vmem((rank, quarter), F32),
            vmem((rank, quarter), F32),
            vmem((RING, rank, quarter), F32),
            vmem((RING, gpart, rank), F32),
            vmem((RING - 1, gpart, rank), F32),
            vmem((gpart, rank), F32),
            vmem((gpart, rank), F32),
            vmem((RING, gpart, rank), F32),
            vmem((rank, rank), F32),
            dma,
        ]
        + [dma(shape) for shape in copies for _ in range(2)],
        compiler_params=pltpu.CompilerParams(
            collective_id=offset, has_side_effects=True, vmem_limit_bytes=40 * 1024 * 1024
        ),
        name="matching",
    )(own, replica)


def first_kernel(w, q, w_out, own):
    value = w[...]
    w_out[...] = value
    high, low = halves(value)
    own[...] = dot(q[0], high, 0, 1) + dot(q[0], low, 0, 1)


def first(replica, factors, tile):
    depth, width = replica.shape
    rank = factors.shape[2]
    return pl.pallas_call(
        first_kernel,
        grid=(depth // tile,),
        out_shape=(
            jax.ShapeDtypeStruct((depth, width), F32),
            jax.ShapeDtypeStruct((rank, depth), F32),
        ),
        in_specs=[
            pl.BlockSpec((tile, width), lambda i: (i, 0)),
            pl.BlockSpec((1, width, rank), lambda i: (0, 0, 0)),
        ],
        out_specs=[
            pl.BlockSpec((tile, width), lambda i: (i, 0)),
            pl.BlockSpec((rank, tile), lambda i: (0, i)),
        ],
        compiler_params=pltpu.CompilerParams(vmem_limit_bytes=32 * 1024 * 1024),
        name="first_left",
    )(replica, factors)


def update_kernel(m, w, xt, st, u, q, w_out, own, s3):
    rank = xt.shape[0]

    @pl.when(pl.program_id(0) == 0)
    def _():
        high, low = halves(st[...])
        s3[:rank] = high
        s3[rank : 2 * rank] = low
        s3[2 * rank :] = high

    high, low = halves(xt[...])
    x3 = jnp.concatenate([high, high, low], axis=0)
    value = w[...] - 0.5 * dot(x3, s3[...], 0, 0)
    last = m[0] == MATCHINGS - 1

    @pl.when(last)
    def _():
        w_out[...] = value
        own[...] = jnp.zeros_like(own)

    @pl.when(jnp.logical_not(last))
    def _():
        stepped = value - u[0].astype(F32)
        w_out[...] = stepped
        high, low = halves(stepped)
        own[...] = dot(q[0], high, 0, 1) + dot(q[0], low, 0, 1)


def update(m, replica, xt, st, updates, factors, tile):
    depth, width = replica.shape
    rank = factors.shape[2]
    top = MATCHINGS - 1
    return pl.pallas_call(
        update_kernel,
        grid_spec=pltpu.PrefetchScalarGridSpec(
            num_scalar_prefetch=1,
            grid=(depth // tile,),
            in_specs=[
                pl.BlockSpec((tile, width), lambda i, m: (i, 0)),
                pl.BlockSpec((rank, tile), lambda i, m: (0, i)),
                pl.BlockSpec((rank, width), lambda i, m: (0, 0)),
                pl.BlockSpec((1, tile, width), lambda i, m: (jnp.minimum(m[0], top - 1), i, 0)),
                pl.BlockSpec((1, width, rank), lambda i, m: (jnp.minimum(m[0] + 1, top), 0, 0)),
            ],
            out_specs=[
                pl.BlockSpec((tile, width), lambda i, m: (i, 0)),
                pl.BlockSpec((rank, tile), lambda i, m: (0, i)),
            ],
            scratch_shapes=[pltpu.VMEM((3 * rank, width), BF16)],
        ),
        out_shape=(
            jax.ShapeDtypeStruct((depth, width), F32),
            jax.ShapeDtypeStruct((rank, depth), F32),
        ),
        input_output_aliases={1: 0},
        compiler_params=pltpu.CompilerParams(vmem_limit_bytes=40 * 1024 * 1024),
        name="apply_step",
    )(jnp.reshape(m, (1,)), replica, xt, st, updates, factors)


def per_device(replicas, weights, updates, factors, partners):
    myself = lax.axis_index("gossip")
    offsets = jnp.bitwise_xor(partners[:, myself], myself)
    tile = min(256, weights.shape[1])
    branches = [functools.partial(phase, offset) for offset in range(1, replicas)]

    def body(m, carry):
        replica, own = carry
        xt, st = lax.switch(offsets[m] - 1, branches, own, replica)
        return update(m, replica, xt, st, updates[0], factors, tile)

    replica, _ = lax.fori_loop(0, MATCHINGS, body, first(weights[0], factors, tile))
    return replica[None]


def solution(mesh):
    placed = (P("gossip", "tensor", None), P("gossip", None, "tensor", None), P(), P())
    return jax.shard_map(
        functools.partial(per_device, mesh.shape["gossip"]),
        mesh=mesh,
        in_specs=placed,
        out_specs=P("gossip", "tensor", None),
        check_vma=False,
    )
```

```python
import functools

import jax
import jax.numpy as jnp
from jax import lax
from jax.experimental import pallas as pl
from jax.experimental.pallas import tpu as pltpu
from jax.sharding import PartitionSpec as P

MATCHINGS = 3
RING = 4
HIGHEST = lax.Precision.HIGHEST
F32 = jnp.float32
BF16 = jnp.bfloat16


def halves(value):
    high = value.astype(BF16)
    return high, (value - high.astype(F32)).astype(BF16)


def dot(first, second, first_dim, second_dim, precision=None):
    return lax.dot_general(
        first,
        second,
        (((first_dim,), (second_dim,)), ((), ())),
        precision=precision,
        preferred_element_type=F32,
    )


def flipped(index, offset):
    bit = 1
    result = index
    while bit <= offset:
        if offset & bit:
            result = result + bit * (1 - 2 * ((index // bit) % 2))
        bit *= 2
    return result


def eliminated(matrix, pivots):
    size = matrix.shape[0]
    lane = lax.broadcasted_iota(jnp.int32, (1, size), 1)
    row_id = lax.broadcasted_iota(jnp.int32, (size, 1), 0)
    columns = [jnp.broadcast_to(matrix[:, j : j + 1], (size, size)) for j in range(pivots)]
    block = [[column[i : i + 1, :] for column in columns] for i in range(pivots)]
    rows = [
        jnp.where(lane < pivots, jnp.where(lane == i, 1.0, 0.0), matrix[i : i + 1, :])
        for i in range(pivots)
    ]
    for k in range(pivots):
        scale = 1.0 / block[k][k]
        rows[k] = rows[k] * scale
        for j in range(k + 1, pivots):
            block[k][j] = block[k][j] * scale
        for i in range(pivots):
            if i != k:
                factor = block[i][k]
                rows[i] = rows[i] - factor * rows[k]
                for j in range(k + 1, pivots):
                    block[i][j] = block[i][j] - factor * block[k][j]
    matrix = jnp.where((lane < pivots) | (row_id < pivots), 0.0, matrix)
    for i in range(pivots):
        taken = jnp.where(row_id == i, -1.0, 0.0)
        matrix = matrix - jnp.where(row_id < pivots, taken, columns[i]) * rows[i]
    return pltpu.roll(pltpu.roll(matrix, size - pivots, 0), size - pivots, 1)


ROOM = 56 * 1024 * 1024


def place():
    g, t = lax.axis_index("gossip"), lax.axis_index("tensor")
    y, zh = t % RING, t // RING
    around = [zh * RING + (y + i) % RING for i in range(RING)]
    return g, t, y, around, (1 - zh) * RING + y


def greet(devices):
    barrier = pltpu.get_barrier_semaphore()
    for device in devices:
        pl.semaphore_signal(barrier, inc=1, device_id=device, device_id_type=pl.DeviceIdType.MESH)
    pl.semaphore_wait(barrier, len(devices))


def remote(src, dst, send, recv, device):
    return pltpu.make_async_remote_copy(
        src_ref=src,
        dst_ref=dst,
        send_sem=send,
        recv_sem=recv,
        device_id=device,
        device_id_type=pl.DeviceIdType.MESH,
    )


def split_into(source, high_ref, low_ref):
    strip = 128

    @pl.loop(0, source.shape[0] // strip)
    def _(s):
        at = pl.ds(pl.multiple_of(s * strip, strip), strip)
        high, low = halves(source[at, :])
        high_ref[at, :] = high
        low_ref[at, :] = low


def sums_kernel(
    own,
    theirs,
    w_hbm,
    xt,
    gram_out,
    summed,
    wf,
    whi,
    wlo,
    rp,
    yr,
    zs,
    zr,
    gp,
    gy,
    gzs,
    gz,
    gf,
    w_sem,
    y_send,
    y_recv,
    z_send,
    z_recv,
    gy_send,
    gy_recv,
    gz_send,
    gz_recv,
    ga_send,
    ga_recv,
):
    rank = own.shape[0]
    quarter = rp.shape[2]
    gpart = rank // RING
    g, t, y, around, across = place()
    order = (2, 1, 3, 0)

    def columns(n):
        return pl.ds(pl.multiple_of(n * quarter, quarter), quarter)

    loads = {
        i: pltpu.make_async_copy(w_hbm.at[:, columns((y + i) % RING)], wf.at[i], w_sem.at[i])
        for i in order
    }
    for i in order:
        loads[i].start()
    greet([(g, around[1]), (g, around[2]), (g, around[3]), (g, across)])
    y_copy = {
        i: remote(rp.at[i], yr.at[i - 1], y_send.at[i - 1], y_recv.at[i - 1], (g, around[i]))
        for i in (2, 1, 3)
    }
    z_copy = remote(zs, zr, z_send, z_recv, (g, across))
    gy_copy = [
        remote(
            gp.at[(y + i) % RING], gy.at[i - 1], gy_send.at[i - 1], gy_recv.at[i - 1], (g, around[i])
        )
        for i in range(1, RING)
    ]
    gz_copy = remote(gzs, gz, gz_send, gz_recv, (g, across))
    ga_copy = [
        remote(gf.at[y], gf.at[y], ga_send.at[i - 1], ga_recv.at[i - 1], (g, around[i]))
        for i in range(1, RING)
    ]

    xt[...] = own[...] - theirs[...]
    gram = dot(xt[...], xt[...], 1, 1, HIGHEST)
    for n in range(RING):
        gp[n] = gram[n * gpart : (n + 1) * gpart]
    for copy in gy_copy:
        copy.start()

    high, low = halves(xt[...])
    both = jnp.concatenate([high, low], axis=0)
    for i in order:
        loads[i].wait()
        split_into(wf.at[i], whi, wlo)
        wide = dot(both, whi[...], 1, 0)
        rp[i] = wide[:rank] + wide[rank:] + dot(high, wlo[...], 1, 0)
        if i:
            y_copy[i].start()
        if i == 3:
            for copy in gy_copy:
                copy.wait_recv()
            gzs[...] = (gp[y] + gy[0]) + (gy[1] + gy[2])
            gz_copy.start()

    for i in (2, 1, 3):
        y_copy[i].wait_recv()
    zs[...] = (rp[0] + yr[0]) + (yr[1] + yr[2])
    z_copy.start()
    gz_copy.wait_recv()
    gf[y] = gzs[...] + gz[...]
    for copy in ga_copy:
        copy.start()
    for copy in ga_copy:
        copy.wait_recv()
    for n in range(RING):
        gram_out[n * gpart : (n + 1) * gpart] = gf[n]
    z_copy.wait_recv()
    summed[...] = zs[...] + zr[...]
    for copy in [*y_copy.values(), z_copy, *gy_copy, gz_copy, *ga_copy]:
        copy.wait_send()


def sums(own, theirs, replica):
    rank, depth = own.shape
    width = replica.shape[1]
    quarter, gpart = width // RING, rank // RING
    dma, vmem = pltpu.SemaphoreType.DMA, pltpu.VMEM
    whole = pl.BlockSpec(memory_space=vmem)
    return pl.pallas_call(
        sums_kernel,
        out_shape=(
            jax.ShapeDtypeStruct((rank, depth), F32),
            jax.ShapeDtypeStruct((rank, rank), F32),
            jax.ShapeDtypeStruct((rank, quarter), F32),
        ),
        in_specs=[whole, whole, pl.BlockSpec(memory_space=pl.ANY)],
        out_specs=[whole, whole, whole],
        scratch_shapes=[
            vmem((RING, depth, quarter), F32),
            vmem((depth, quarter), BF16),
            vmem((depth, quarter), BF16),
            vmem((RING, rank, quarter), F32),
            vmem((RING - 1, rank, quarter), F32),
            vmem((rank, quarter), F32),
            vmem((rank, quarter), F32),
            vmem((RING, gpart, rank), F32),
            vmem((RING - 1, gpart, rank), F32),
            vmem((gpart, rank), F32),
            vmem((gpart, rank), F32),
            vmem((RING, gpart, rank), F32),
            dma((RING,)),
        ]
        + [dma(shape) for shape in [(3,), (), (3,), (), (3,)] for _ in range(2)],
        compiler_params=pltpu.CompilerParams(
            collective_id=0, has_side_effects=True, vmem_limit_bytes=ROOM
        ),
        name="sums",
    )(own, theirs, replica)


def step_kernel(m, summed, other, gram, xt, w_hbm, *refs):
    if m < MATCHINGS - 1:
        u_hbm, q_ref, w_out, own, wf, uf, inv, s3, x3, rs, rr, w_sem, u_sem, o_sem, a_send, a_recv = refs
    else:
        w_out, wf, inv, s3, x3, rs, rr, w_sem, o_sem, a_send, a_recv = refs
    rank, depth = xt.shape
    quarter = rs.shape[1]
    g, _, y, around, _ = place()
    order = (0, 1, 3, 2)

    def columns(i):
        n = (y + RING - i) % RING
        return pl.ds(pl.multiple_of(n * quarter, quarter), quarter)

    loads = {}
    for i in order:
        loads[i] = [pltpu.make_async_copy(w_hbm.at[:, columns(i)], wf.at[i], w_sem.at[i])]
        if m < MATCHINGS - 1:
            loads[i].append(
                pltpu.make_async_copy(u_hbm.at[m, :, columns(i)], uf.at[i], u_sem.at[i])
            )
        for copy in loads[i]:
            copy.start()
    greet([(g, around[1]), (g, around[2]), (g, around[3])])
    rs[...] = summed[...] + other[...]
    a_copy = {
        i: remote(rs, rr.at[i - 1], a_send.at[i - 1], a_recv.at[i - 1], (g, around[i]))
        for i in (2, 1, 3)
    }
    for copy in a_copy.values():
        copy.start()

    high, low = halves(xt[...])
    x3[:rank] = high
    x3[rank : 2 * rank] = high
    x3[2 * rank :] = low
    inv[...] = gram[...]
    inv[...] = lax.fori_loop(0, rank // 8, lambda _, v: eliminated(v, 8), inv[...])

    stores = []
    for i in order:
        if i:
            a_copy[i].wait_recv()
        right = rs[...] if i == 0 else rr[i - 1]
        high, low = halves(0.5 * dot(inv[...], right, 1, 0, HIGHEST))
        s3[:rank] = high
        s3[rank : 2 * rank] = low
        s3[2 * rank :] = high
        for copy in loads[i]:
            copy.wait()
        value = wf[i] - dot(x3[...], s3[...], 0, 0)
        if m < MATCHINGS - 1:
            value = value - uf[i].astype(F32)
            high, low = halves(value)
            q = q_ref[m + 1, columns(i), :]
            more = dot(q, high, 0, 1) + dot(q, low, 0, 1)
            own[...] = more if i == 0 else own[...] + more
        wf[i] = value
        stores.append(pltpu.make_async_copy(wf.at[i], w_out.at[:, columns(i)], o_sem.at[i]))
        stores[-1].start()
    for copy in stores:
        copy.wait()
    for copy in a_copy.values():
        copy.wait_send()


def step(m, summed, other, gram, xt, replica, updates, factors):
    rank, depth = xt.shape
    width = replica.shape[1]
    quarter = width // RING
    dma, vmem = pltpu.SemaphoreType.DMA, pltpu.VMEM
    whole, anywhere = pl.BlockSpec(memory_space=vmem), pl.BlockSpec(memory_space=pl.ANY)
    more = m < MATCHINGS - 1
    operands = [summed, other, gram, xt, replica]
    in_specs = [whole] * 4 + [anywhere]
    out_shape = [jax.ShapeDtypeStruct((depth, width), F32)]
    out_specs = [anywhere]
    scratch = [vmem((RING, depth, quarter), F32)]
    if more:
        operands += [updates, factors]
        in_specs += [anywhere, whole]
        out_shape += [jax.ShapeDtypeStruct((rank, depth), F32)]
        out_specs += [whole]
        scratch += [vmem((RING, depth, quarter), BF16)]
    scratch += [
        vmem((rank, rank), F32),
        vmem((3 * rank, quarter), BF16),
        vmem((3 * rank, depth), BF16),
        vmem((rank, quarter), F32),
        vmem((RING - 1, rank, quarter), F32),
    ]
    scratch += [dma((RING,))] * (3 if more else 2) + [dma((3,))] * 2
    return pl.pallas_call(
        functools.partial(step_kernel, m),
        out_shape=tuple(out_shape),
        in_specs=in_specs,
        out_specs=out_specs,
        scratch_shapes=scratch,
        compiler_params=pltpu.CompilerParams(
            collective_id=1 + m, has_side_effects=True, vmem_limit_bytes=ROOM
        ),
        name="apply_step",
    )(*operands)


def first_kernel(w, q, own):
    high, low = halves(w[...])
    own[...] = dot(q[...], high, 0, 1) + dot(q[...], low, 0, 1)


def first(replica, factors):
    depth, width = replica.shape
    rank = factors.shape[2]
    tile = min(256, depth)
    return pl.pallas_call(
        first_kernel,
        grid=(depth // tile,),
        out_shape=jax.ShapeDtypeStruct((rank, depth), F32),
        in_specs=[
            pl.BlockSpec((tile, width), lambda i: (i, 0)),
            pl.BlockSpec((None, width, rank), lambda i: (0, 0, 0)),
        ],
        out_specs=pl.BlockSpec((rank, tile), lambda i: (0, i)),
        compiler_params=pltpu.CompilerParams(vmem_limit_bytes=ROOM),
        name="first_left",
    )(replica, factors)


def moved(value, offset):
    pairs = [(i, i ^ offset) for i in range(lax.axis_size("gossip"))]
    return lax.ppermute(value, "gossip", pairs)


def from_mate(value, offset, replicas):
    branches = [functools.partial(moved, offset=c) for c in range(1, replicas)]
    return lax.switch(offset - 1, branches, value)


def per_device(replicas, weights, updates, factors, partners):
    myself = lax.axis_index("gossip")
    offsets = jnp.bitwise_xor(partners[:, myself], myself)
    replica = weights[0]
    own = first(replica, factors)
    for m in range(MATCHINGS):
        theirs = from_mate(own, offsets[m], replicas)
        xt, gram, summed = sums(own, theirs, replica)
        other = from_mate(summed, offsets[m], replicas)
        replica, *rest = step(m, summed, other, gram, xt, replica, updates[0], factors)
        own = rest[0] if rest else None
    return replica[None]


def solution(mesh):
    placed = (P("gossip", "tensor", None), P("gossip", None, "tensor", None), P(), P())
    return jax.shard_map(
        functools.partial(per_device, mesh.shape["gossip"]),
        mesh=mesh,
        in_specs=placed,
        out_specs=P("gossip", "tensor", None),
        check_vma=False,
    )
```

```python
import functools

import jax
import jax.numpy as jnp
from jax import lax
from jax.experimental import pallas as pl
from jax.experimental.pallas import tpu as pltpu
from jax.sharding import PartitionSpec as P

MATCHINGS = 3
RING = 4
HIGHEST = lax.Precision.HIGHEST
F32 = jnp.float32
BF16 = jnp.bfloat16


def halves(value):
    high = value.astype(BF16)
    return high, (value - high.astype(F32)).astype(BF16)


def dot(first, second, first_dim, second_dim, precision=None):
    return lax.dot_general(
        first,
        second,
        (((first_dim,), (second_dim,)), ((), ())),
        precision=precision,
        preferred_element_type=F32,
    )


def flipped(index, offset):
    bit = 1
    result = index
    while bit <= offset:
        if offset & bit:
            result = result + bit * (1 - 2 * ((index // bit) % 2))
        bit *= 2
    return result


def eliminated(matrix, pivots):
    size = matrix.shape[0]
    lane = lax.broadcasted_iota(jnp.int32, (1, size), 1)
    row_id = lax.broadcasted_iota(jnp.int32, (size, 1), 0)
    columns = [jnp.broadcast_to(matrix[:, j : j + 1], (size, size)) for j in range(pivots)]
    block = [[column[i : i + 1, :] for column in columns] for i in range(pivots)]
    rows = [
        jnp.where(lane < pivots, jnp.where(lane == i, 1.0, 0.0), matrix[i : i + 1, :])
        for i in range(pivots)
    ]
    for k in range(pivots):
        scale = 1.0 / block[k][k]
        rows[k] = rows[k] * scale
        for j in range(k + 1, pivots):
            block[k][j] = block[k][j] * scale
        for i in range(pivots):
            if i != k:
                factor = block[i][k]
                rows[i] = rows[i] - factor * rows[k]
                for j in range(k + 1, pivots):
                    block[i][j] = block[i][j] - factor * block[k][j]
    matrix = jnp.where((lane < pivots) | (row_id < pivots), 0.0, matrix)
    for i in range(pivots):
        taken = jnp.where(row_id == i, -1.0, 0.0)
        matrix = matrix - jnp.where(row_id < pivots, taken, columns[i]) * rows[i]
    return pltpu.roll(pltpu.roll(matrix, size - pivots, 0), size - pivots, 1)


ROOM = 56 * 1024 * 1024


def place():
    g, t = lax.axis_index("gossip"), lax.axis_index("tensor")
    y, zh = t % RING, t // RING
    around = [zh * RING + (y + i) % RING for i in range(RING)]
    return g, t, y, around, (1 - zh) * RING + y


def greet(devices):
    barrier = pltpu.get_barrier_semaphore()
    for device in devices:
        pl.semaphore_signal(barrier, inc=1, device_id=device, device_id_type=pl.DeviceIdType.MESH)
    return lambda: pl.semaphore_wait(barrier, len(devices))


def remote(src, dst, send, recv, device):
    return pltpu.make_async_remote_copy(
        src_ref=src,
        dst_ref=dst,
        send_sem=send,
        recv_sem=recv,
        device_id=device,
        device_id_type=pl.DeviceIdType.MESH,
    )


def split_into(source, high_ref, low_ref):
    strip = 128

    @pl.loop(0, source.shape[0] // strip)
    def _(s):
        at = pl.ds(pl.multiple_of(s * strip, strip), strip)
        high, low = halves(source[at, :])
        high_ref[at, :] = high
        low_ref[at, :] = low


def sums_kernel(
    own,
    theirs,
    w_hbm,
    xt,
    gram_out,
    summed,
    wf,
    whi,
    wlo,
    rp,
    yr,
    zs,
    zr,
    gp,
    gy,
    gzs,
    gz,
    gf,
    w_sem,
    y_send,
    y_recv,
    z_send,
    z_recv,
    gy_send,
    gy_recv,
    gz_send,
    gz_recv,
    ga_send,
    ga_recv,
):
    rank = own.shape[0]
    quarter = rp.shape[2]
    gpart = rank // RING
    g, t, y, around, across = place()
    order = (2, 1, 3, 0)

    def columns(n):
        return pl.ds(pl.multiple_of(n * quarter, quarter), quarter)

    loads = {
        i: pltpu.make_async_copy(w_hbm.at[:, columns((y + i) % RING)], wf.at[i], w_sem.at[i])
        for i in order
    }
    for i in order:
        loads[i].start()
    all_here = greet([(g, around[1]), (g, around[2]), (g, around[3]), (g, across)])
    y_copy = {
        i: remote(rp.at[i], yr.at[i - 1], y_send.at[i - 1], y_recv.at[i - 1], (g, around[i]))
        for i in (2, 1, 3)
    }
    z_copy = remote(zs, zr, z_send, z_recv, (g, across))
    gy_copy = [
        remote(
            gp.at[(y + i) % RING], gy.at[i - 1], gy_send.at[i - 1], gy_recv.at[i - 1], (g, around[i])
        )
        for i in range(1, RING)
    ]
    gz_copy = remote(gzs, gz, gz_send, gz_recv, (g, across))
    ga_copy = [
        remote(gf.at[y], gf.at[y], ga_send.at[i - 1], ga_recv.at[i - 1], (g, around[i]))
        for i in range(1, RING)
    ]

    xt[...] = own[...] - theirs[...]
    high, low = halves(xt[...])
    both = jnp.concatenate([high, low], axis=0)

    def product(i):
        loads[i].wait()
        split_into(wf.at[i], whi, wlo)
        wide = dot(both, whi[...], 1, 0)
        rp[i] = wide[:rank] + wide[rank:] + dot(high, wlo[...], 1, 0)

    for i in (2, 1, 3):
        product(i)
        if i == 2:
            all_here()
        y_copy[i].start()
    gram = dot(xt[...], xt[...], 1, 1, HIGHEST)
    for n in range(RING):
        gp[n] = gram[n * gpart : (n + 1) * gpart]
    for copy in gy_copy:
        copy.start()
    product(0)

    for copy in gy_copy:
        copy.wait_recv()
    gzs[...] = (gp[y] + gy[0]) + (gy[1] + gy[2])
    gz_copy.start()
    for i in (2, 1, 3):
        y_copy[i].wait_recv()
    zs[...] = (rp[0] + yr[0]) + (yr[1] + yr[2])
    z_copy.start()
    gz_copy.wait_recv()
    gf[y] = gzs[...] + gz[...]
    for copy in ga_copy:
        copy.start()
    for copy in ga_copy:
        copy.wait_recv()
    for n in range(RING):
        gram_out[n * gpart : (n + 1) * gpart] = gf[n]
    z_copy.wait_recv()
    summed[...] = zs[...] + zr[...]
    for copy in [*y_copy.values(), z_copy, *gy_copy, gz_copy, *ga_copy]:
        copy.wait_send()


def sums(own, theirs, replica):
    rank, depth = own.shape
    width = replica.shape[1]
    quarter, gpart = width // RING, rank // RING
    dma, vmem = pltpu.SemaphoreType.DMA, pltpu.VMEM
    whole = pl.BlockSpec(memory_space=vmem)
    return pl.pallas_call(
        sums_kernel,
        out_shape=(
            jax.ShapeDtypeStruct((rank, depth), F32),
            jax.ShapeDtypeStruct((rank, rank), F32),
            jax.ShapeDtypeStruct((rank, quarter), F32),
        ),
        in_specs=[whole, whole, pl.BlockSpec(memory_space=pl.ANY)],
        out_specs=[whole, whole, whole],
        scratch_shapes=[
            vmem((RING, depth, quarter), F32),
            vmem((depth, quarter), BF16),
            vmem((depth, quarter), BF16),
            vmem((RING, rank, quarter), F32),
            vmem((RING - 1, rank, quarter), F32),
            vmem((rank, quarter), F32),
            vmem((rank, quarter), F32),
            vmem((RING, gpart, rank), F32),
            vmem((RING - 1, gpart, rank), F32),
            vmem((gpart, rank), F32),
            vmem((gpart, rank), F32),
            vmem((RING, gpart, rank), F32),
            dma((RING,)),
        ]
        + [dma(shape) for shape in [(3,), (), (3,), (), (3,)] for _ in range(2)],
        compiler_params=pltpu.CompilerParams(
            collective_id=0, has_side_effects=True, vmem_limit_bytes=ROOM
        ),
        name="sums",
    )(own, theirs, replica)


def step_kernel(m, summed, other, gram, xt, w_hbm, *refs):
    if m < MATCHINGS - 1:
        u_hbm, q_ref, w_out, own, wf, uf, inv, s3, x3, rs, rr, w_sem, u_sem, o_sem, a_send, a_recv = refs
    else:
        w_out, wf, inv, s3, x3, rs, rr, w_sem, o_sem, a_send, a_recv = refs
    rank, depth = xt.shape
    quarter = rs.shape[1]
    g, _, y, around, _ = place()
    order = (0, 1, 3, 2)

    def columns(i):
        n = (y + RING - i) % RING
        return pl.ds(pl.multiple_of(n * quarter, quarter), quarter)

    loads = {}
    for i in order:
        loads[i] = [pltpu.make_async_copy(w_hbm.at[:, columns(i)], wf.at[i], w_sem.at[i])]
        if m < MATCHINGS - 1:
            loads[i].append(
                pltpu.make_async_copy(u_hbm.at[m, :, columns(i)], uf.at[i], u_sem.at[i])
            )
        for copy in loads[i]:
            copy.start()
    all_here = greet([(g, around[1]), (g, around[2]), (g, around[3])])
    rs[...] = summed[...] + other[...]
    a_copy = {
        i: remote(rs, rr.at[i - 1], a_send.at[i - 1], a_recv.at[i - 1], (g, around[i]))
        for i in (2, 1, 3)
    }
    all_here()
    for copy in a_copy.values():
        copy.start()

    high, low = halves(xt[...])
    x3[:rank] = high
    x3[rank : 2 * rank] = high
    x3[2 * rank :] = low
    inv[...] = gram[...]
    inv[...] = lax.fori_loop(0, rank // 8, lambda _, v: eliminated(v, 8), inv[...])

    stores = []
    for i in order:
        if i:
            a_copy[i].wait_recv()
        right = rs[...] if i == 0 else rr[i - 1]
        high, low = halves(0.5 * dot(inv[...], right, 1, 0, HIGHEST))
        s3[:rank] = high
        s3[rank : 2 * rank] = low
        s3[2 * rank :] = high
        for copy in loads[i]:
            copy.wait()
        value = wf[i] - dot(x3[...], s3[...], 0, 0)
        if m < MATCHINGS - 1:
            value = value - uf[i].astype(F32)
            high, low = halves(value)
            q = q_ref[m + 1, columns(i), :]
            more = dot(q, high, 0, 1) + dot(q, low, 0, 1)
            own[...] = more if i == 0 else own[...] + more
        wf[i] = value
        stores.append(pltpu.make_async_copy(wf.at[i], w_out.at[:, columns(i)], o_sem.at[i]))
        stores[-1].start()
    for copy in stores:
        copy.wait()
    for copy in a_copy.values():
        copy.wait_send()


def step(m, summed, other, gram, xt, replica, updates, factors):
    rank, depth = xt.shape
    width = replica.shape[1]
    quarter = width // RING
    dma, vmem = pltpu.SemaphoreType.DMA, pltpu.VMEM
    whole, anywhere = pl.BlockSpec(memory_space=vmem), pl.BlockSpec(memory_space=pl.ANY)
    more = m < MATCHINGS - 1
    operands = [summed, other, gram, xt, replica]
    in_specs = [whole] * 4 + [anywhere]
    out_shape = [jax.ShapeDtypeStruct((depth, width), F32)]
    out_specs = [anywhere]
    scratch = [vmem((RING, depth, quarter), F32)]
    if more:
        operands += [updates, factors]
        in_specs += [anywhere, whole]
        out_shape += [jax.ShapeDtypeStruct((rank, depth), F32)]
        out_specs += [whole]
        scratch += [vmem((RING, depth, quarter), BF16)]
    scratch += [
        vmem((rank, rank), F32),
        vmem((3 * rank, quarter), BF16),
        vmem((3 * rank, depth), BF16),
        vmem((rank, quarter), F32),
        vmem((RING - 1, rank, quarter), F32),
    ]
    scratch += [dma((RING,))] * (3 if more else 2) + [dma((3,))] * 2
    return pl.pallas_call(
        functools.partial(step_kernel, m),
        out_shape=tuple(out_shape),
        in_specs=in_specs,
        out_specs=out_specs,
        scratch_shapes=scratch,
        compiler_params=pltpu.CompilerParams(
            collective_id=1 + m, has_side_effects=True, vmem_limit_bytes=ROOM
        ),
        name="apply_step",
    )(*operands)


def first_kernel(w, q, own):
    high, low = halves(w[...])
    own[...] = dot(q[...], high, 0, 1) + dot(q[...], low, 0, 1)


def first(replica, factors):
    depth, width = replica.shape
    rank = factors.shape[2]
    tile = min(256, depth)
    return pl.pallas_call(
        first_kernel,
        grid=(depth // tile,),
        out_shape=jax.ShapeDtypeStruct((rank, depth), F32),
        in_specs=[
            pl.BlockSpec((tile, width), lambda i: (i, 0)),
            pl.BlockSpec((None, width, rank), lambda i: (0, 0, 0)),
        ],
        out_specs=pl.BlockSpec((rank, tile), lambda i: (0, i)),
        compiler_params=pltpu.CompilerParams(vmem_limit_bytes=ROOM),
        name="first_left",
    )(replica, factors)


def moved(value, offset):
    pairs = [(i, i ^ offset) for i in range(lax.axis_size("gossip"))]
    return lax.ppermute(value, "gossip", pairs)


def from_mate(value, offset, replicas):
    branches = [functools.partial(moved, offset=c) for c in range(1, replicas)]
    return lax.switch(offset - 1, branches, value)


def per_device(replicas, weights, updates, factors, partners):
    offsets = partners[:, 0]
    replica = weights[0]
    own = first(replica, factors)
    for m in range(MATCHINGS):
        theirs = from_mate(own, offsets[m], replicas)
        xt, gram, summed = sums(own, theirs, replica)
        other = from_mate(summed, offsets[m], replicas)
        replica, *rest = step(m, summed, other, gram, xt, replica, updates[0], factors)
        own = rest[0] if rest else None
    return replica[None]


def solution(mesh):
    placed = (P("gossip", "tensor", None), P("gossip", None, "tensor", None), P(), P())
    return jax.shard_map(
        functools.partial(per_device, mesh.shape["gossip"]),
        mesh=mesh,
        in_specs=placed,
        out_specs=P("gossip", "tensor", None),
        check_vma=False,
    )
```

```python
import functools

import jax
import jax.numpy as jnp
from jax import lax
from jax.experimental import pallas as pl
from jax.experimental.pallas import tpu as pltpu
from jax.sharding import PartitionSpec as P

MATCHINGS = 3
RING = 4
HIGHEST = lax.Precision.HIGHEST
F32 = jnp.float32
BF16 = jnp.bfloat16


def halves(value):
    high = value.astype(BF16)
    return high, (value - high.astype(F32)).astype(BF16)


def dot(first, second, first_dim, second_dim, precision=None):
    return lax.dot_general(
        first,
        second,
        (((first_dim,), (second_dim,)), ((), ())),
        precision=precision,
        preferred_element_type=F32,
    )


def flipped(index, offset):
    bit = 1
    result = index
    while bit <= offset:
        if offset & bit:
            result = result + bit * (1 - 2 * ((index // bit) % 2))
        bit *= 2
    return result


def eliminated(matrix, pivots):
    size = matrix.shape[0]
    lane = lax.broadcasted_iota(jnp.int32, (1, size), 1)
    row_id = lax.broadcasted_iota(jnp.int32, (size, 1), 0)
    columns = [jnp.broadcast_to(matrix[:, j : j + 1], (size, size)) for j in range(pivots)]
    block = [[column[i : i + 1, :] for column in columns] for i in range(pivots)]
    rows = [
        jnp.where(lane < pivots, jnp.where(lane == i, 1.0, 0.0), matrix[i : i + 1, :])
        for i in range(pivots)
    ]
    for k in range(pivots):
        scale = 1.0 / block[k][k]
        rows[k] = rows[k] * scale
        for j in range(k + 1, pivots):
            block[k][j] = block[k][j] * scale
        for i in range(pivots):
            if i != k:
                factor = block[i][k]
                rows[i] = rows[i] - factor * rows[k]
                for j in range(k + 1, pivots):
                    block[i][j] = block[i][j] - factor * block[k][j]
    matrix = jnp.where((lane < pivots) | (row_id < pivots), 0.0, matrix)
    for i in range(pivots):
        taken = jnp.where(row_id == i, -1.0, 0.0)
        matrix = matrix - jnp.where(row_id < pivots, taken, columns[i]) * rows[i]
    return pltpu.roll(pltpu.roll(matrix, size - pivots, 0), size - pivots, 1)


ROOM = 56 * 1024 * 1024


def place():
    g, t = lax.axis_index("gossip"), lax.axis_index("tensor")
    y, zh = t % RING, t // RING
    around = [zh * RING + (y + i) % RING for i in range(RING)]
    return g, t, y, around, (1 - zh) * RING + y


def greet(devices):
    barrier = pltpu.get_barrier_semaphore()
    for device in devices:
        pl.semaphore_signal(barrier, inc=1, device_id=device, device_id_type=pl.DeviceIdType.MESH)
    return lambda: pl.semaphore_wait(barrier, len(devices))


def remote(src, dst, send, recv, device):
    return pltpu.make_async_remote_copy(
        src_ref=src,
        dst_ref=dst,
        send_sem=send,
        recv_sem=recv,
        device_id=device,
        device_id_type=pl.DeviceIdType.MESH,
    )


def split_into(source, high_ref, low_ref):
    strip = 128

    @pl.loop(0, source.shape[0] // strip)
    def _(s):
        at = pl.ds(pl.multiple_of(s * strip, strip), strip)
        high, low = halves(source[at, :])
        high_ref[at, :] = high
        low_ref[at, :] = low


def sums_kernel(
    own,
    theirs,
    w_hbm,
    xt,
    gram_out,
    summed,
    wf,
    whi,
    wlo,
    rp,
    yr,
    zs,
    zr,
    gp,
    gy,
    gzs,
    gz,
    gf,
    w_sem,
    y_send,
    y_recv,
    z_send,
    z_recv,
    gy_send,
    gy_recv,
    gz_send,
    gz_recv,
    ga_send,
    ga_recv,
):
    rank = own.shape[0]
    quarter = rp.shape[2]
    gpart = rank // RING
    g, t, y, around, across = place()
    order = (2, 1, 3, 0)

    def columns(n):
        return pl.ds(pl.multiple_of(n * quarter, quarter), quarter)

    loads = {
        i: pltpu.make_async_copy(w_hbm.at[:, columns((y + i) % RING)], wf.at[i], w_sem.at[i])
        for i in order
    }
    for i in order:
        loads[i].start()
    all_here = greet([(g, around[1]), (g, around[2]), (g, around[3]), (g, across)])
    y_copy = {
        i: remote(rp.at[i], yr.at[i - 1], y_send.at[i - 1], y_recv.at[i - 1], (g, around[i]))
        for i in (2, 1, 3)
    }
    z_copy = remote(zs, zr, z_send, z_recv, (g, across))
    gy_copy = [
        remote(
            gp.at[(y + i) % RING], gy.at[i - 1], gy_send.at[i - 1], gy_recv.at[i - 1], (g, around[i])
        )
        for i in range(1, RING)
    ]
    gz_copy = remote(gzs, gz, gz_send, gz_recv, (g, across))
    ga_copy = [
        remote(gf.at[y], gf.at[y], ga_send.at[i - 1], ga_recv.at[i - 1], (g, around[i]))
        for i in range(1, RING)
    ]

    xt[...] = own[...] - theirs[...]
    high, low = halves(xt[...])
    both = jnp.concatenate([high, low], axis=0)

    def product(i):
        loads[i].wait()
        split_into(wf.at[i], whi, wlo)
        wide = dot(both, whi[...], 1, 0)
        rp[i] = wide[:rank] + wide[rank:] + dot(high, wlo[...], 1, 0)

    for i in (2, 1, 3):
        product(i)
        if i == 2:
            all_here()
        y_copy[i].start()
    gram = dot(xt[...], xt[...], 1, 1, HIGHEST)
    for n in range(RING):
        gp[n] = gram[n * gpart : (n + 1) * gpart]
    for copy in gy_copy:
        copy.start()
    product(0)

    for copy in gy_copy:
        copy.wait_recv()
    gzs[...] = (gp[y] + gy[0]) + (gy[1] + gy[2])
    gz_copy.start()
    for i in (2, 1, 3):
        y_copy[i].wait_recv()
    zs[...] = (rp[0] + yr[0]) + (yr[1] + yr[2])
    z_copy.start()
    gz_copy.wait_recv()
    gf[y] = gzs[...] + gz[...]
    for copy in ga_copy:
        copy.start()
    for copy in ga_copy:
        copy.wait_recv()
    for n in range(RING):
        gram_out[n * gpart : (n + 1) * gpart] = gf[n]
    z_copy.wait_recv()
    summed[...] = zs[...] + zr[...]
    for copy in [*y_copy.values(), z_copy, *gy_copy, gz_copy, *ga_copy]:
        copy.wait_send()


def sums(own, theirs, replica):
    rank, depth = own.shape
    width = replica.shape[1]
    quarter, gpart = width // RING, rank // RING
    dma, vmem = pltpu.SemaphoreType.DMA, pltpu.VMEM
    whole = pl.BlockSpec(memory_space=vmem)
    return pl.pallas_call(
        sums_kernel,
        out_shape=(
            jax.ShapeDtypeStruct((rank, depth), F32),
            jax.ShapeDtypeStruct((rank, rank), F32),
            jax.ShapeDtypeStruct((rank, quarter), F32),
        ),
        in_specs=[whole, whole, pl.BlockSpec(memory_space=pl.ANY)],
        out_specs=[whole, whole, whole],
        scratch_shapes=[
            vmem((RING, depth, quarter), F32),
            vmem((depth, quarter), BF16),
            vmem((depth, quarter), BF16),
            vmem((RING, rank, quarter), F32),
            vmem((RING - 1, rank, quarter), F32),
            vmem((rank, quarter), F32),
            vmem((rank, quarter), F32),
            vmem((RING, gpart, rank), F32),
            vmem((RING - 1, gpart, rank), F32),
            vmem((gpart, rank), F32),
            vmem((gpart, rank), F32),
            vmem((RING, gpart, rank), F32),
            dma((RING,)),
        ]
        + [dma(shape) for shape in [(3,), (), (3,), (), (3,)] for _ in range(2)],
        compiler_params=pltpu.CompilerParams(
            collective_id=0, has_side_effects=True, vmem_limit_bytes=ROOM
        ),
        name="sums",
    )(own, theirs, replica)


def step_kernel(m, summed, other, gram, xt, w_hbm, *refs):
    if m < MATCHINGS - 1:
        u_hbm, q_ref, w_out, own, wf, uf, inv, s3, x3, rs, rr, w_sem, u_sem, o_sem, a_send, a_recv = refs
    else:
        w_out, wf, inv, s3, x3, rs, rr, w_sem, o_sem, a_send, a_recv = refs
    rank, depth = xt.shape
    quarter = rs.shape[1]
    g, _, y, around, _ = place()
    order = (0, 1, 3, 2)

    def columns(i):
        n = (y + RING - i) % RING
        return pl.ds(pl.multiple_of(n * quarter, quarter), quarter)

    loads = {}
    for i in order:
        loads[i] = [pltpu.make_async_copy(w_hbm.at[:, columns(i)], wf.at[i], w_sem.at[i])]
        if m < MATCHINGS - 1:
            loads[i].append(
                pltpu.make_async_copy(u_hbm.at[m, :, columns(i)], uf.at[i], u_sem.at[i])
            )
        for copy in loads[i]:
            copy.start()
    all_here = greet([(g, around[1]), (g, around[2]), (g, around[3])])
    rs[...] = summed[...] + other[...]
    a_copy = {
        i: remote(rs, rr.at[i - 1], a_send.at[i - 1], a_recv.at[i - 1], (g, around[i]))
        for i in (2, 1, 3)
    }
    high, low = halves(xt[...])
    x3[:rank] = high
    x3[rank : 2 * rank] = high
    x3[2 * rank :] = low
    all_here()
    for copy in a_copy.values():
        copy.start()

    inv[...] = gram[...]
    inv[...] = lax.fori_loop(0, rank // 8, lambda _, v: eliminated(v, 8), inv[...])

    stores = []
    for i in order:
        if i:
            a_copy[i].wait_recv()
        right = rs[...] if i == 0 else rr[i - 1]
        high, low = halves(0.5 * dot(inv[...], right, 1, 0, HIGHEST))
        s3[:rank] = high
        s3[rank : 2 * rank] = low
        s3[2 * rank :] = high
        for copy in loads[i]:
            copy.wait()
        value = wf[i] - dot(x3[...], s3[...], 0, 0)
        if m < MATCHINGS - 1:
            value = value - uf[i].astype(F32)
            high, low = halves(value)
            q = q_ref[m + 1, columns(i), :]
            more = dot(q, high, 0, 1) + dot(q, low, 0, 1)
            own[...] = more if i == 0 else own[...] + more
        wf[i] = value
        stores.append(pltpu.make_async_copy(wf.at[i], w_out.at[:, columns(i)], o_sem.at[i]))
        stores[-1].start()
    for copy in stores:
        copy.wait()
    for copy in a_copy.values():
        copy.wait_send()


def step(m, summed, other, gram, xt, replica, updates, factors):
    rank, depth = xt.shape
    width = replica.shape[1]
    quarter = width // RING
    dma, vmem = pltpu.SemaphoreType.DMA, pltpu.VMEM
    whole, anywhere = pl.BlockSpec(memory_space=vmem), pl.BlockSpec(memory_space=pl.ANY)
    more = m < MATCHINGS - 1
    operands = [summed, other, gram, xt, replica]
    in_specs = [whole] * 4 + [anywhere]
    out_shape = [jax.ShapeDtypeStruct((depth, width), F32)]
    out_specs = [anywhere]
    scratch = [vmem((RING, depth, quarter), F32)]
    if more:
        operands += [updates, factors]
        in_specs += [anywhere, whole]
        out_shape += [jax.ShapeDtypeStruct((rank, depth), F32)]
        out_specs += [whole]
        scratch += [vmem((RING, depth, quarter), BF16)]
    scratch += [
        vmem((rank, rank), F32),
        vmem((3 * rank, quarter), BF16),
        vmem((3 * rank, depth), BF16),
        vmem((rank, quarter), F32),
        vmem((RING - 1, rank, quarter), F32),
    ]
    scratch += [dma((RING,))] * (3 if more else 2) + [dma((3,))] * 2
    return pl.pallas_call(
        functools.partial(step_kernel, m),
        out_shape=tuple(out_shape),
        in_specs=in_specs,
        out_specs=out_specs,
        scratch_shapes=scratch,
        compiler_params=pltpu.CompilerParams(
            collective_id=1 + m, has_side_effects=True, vmem_limit_bytes=ROOM
        ),
        name="apply_step",
    )(*operands)


def first_kernel(w, q, own):
    high, low = halves(w[...])
    own[...] = dot(q[...], high, 0, 1) + dot(q[...], low, 0, 1)


def first(replica, factors):
    depth, width = replica.shape
    rank = factors.shape[2]
    tile = min(512, depth)
    return pl.pallas_call(
        first_kernel,
        grid=(depth // tile,),
        out_shape=jax.ShapeDtypeStruct((rank, depth), F32),
        in_specs=[
            pl.BlockSpec((tile, width), lambda i: (i, 0)),
            pl.BlockSpec((None, width, rank), lambda i: (0, 0, 0)),
        ],
        out_specs=pl.BlockSpec((rank, tile), lambda i: (0, i)),
        compiler_params=pltpu.CompilerParams(vmem_limit_bytes=ROOM),
        name="first_left",
    )(replica, factors)


def moved(value, offset):
    pairs = [(i, i ^ offset) for i in range(lax.axis_size("gossip"))]
    return lax.ppermute(value, "gossip", pairs)


def from_mate(value, offset, replicas):
    branches = [functools.partial(moved, offset=c) for c in range(1, replicas)]
    return lax.switch(offset - 1, branches, value)


def per_device(replicas, weights, updates, factors, partners):
    offsets = partners[:, 0]
    replica = weights[0]
    own = first(replica, factors)
    for m in range(MATCHINGS):
        theirs = from_mate(own, offsets[m], replicas)
        xt, gram, summed = sums(own, theirs, replica)
        other = from_mate(summed, offsets[m], replicas)
        replica, *rest = step(m, summed, other, gram, xt, replica, updates[0], factors)
        own = rest[0] if rest else None
    return replica[None]


def solution(mesh):
    placed = (P("gossip", "tensor", None), P("gossip", None, "tensor", None), P(), P())
    return jax.shard_map(
        functools.partial(per_device, mesh.shape["gossip"]),
        mesh=mesh,
        in_specs=placed,
        out_specs=P("gossip", "tensor", None),
        check_vma=False,
    )
```
